128 devices in a mesh: prompt: 8 (over y, x_lo), comp: 16 (over z, x_hi, core).
Axes of the slice: x: 4 (x_hi: 2, x_lo: 2; x = x_hi * 2 + x_lo), y: 4, z: 4, core: 2. Of those that a mesh axis runs over, the one named last changes fastest.
Arguments:
- q_nope: bfloat16 [2048, 16384], P('comp', 'prompt'), may hold values from -6 to 6
- q_rope: bfloat16 [2048, 8192], P('comp', 'prompt'), may hold values from -250 to 250
- d_out: bfloat16 [2048, 16384], P('comp', 'prompt'), may hold values from -6 to 6
- w_uk: bfloat16 [128, 128, 512], P('prompt'), may hold values from -0.5 to 0.5
- w_uv: bfloat16 [128, 512, 128], P('prompt'), may hold values from -0.25 to 0.25
- latent: bfloat16 [1024, 512], P('prompt'), may hold values from -6 to 6
- rope_key: bfloat16 [1024, 64], P('prompt'), may hold values from -5 to 5
- comp_latent: bfloat16 [2048, 512], P('comp'), may hold values from -6 to 6
- comp_rope: bfloat16 [2048, 64], P('comp'), may hold values from -6 to 6
- lengths: int32 [32], P('comp'), may hold values from 1 to 64
Outputs:
- d_w_uk: float32 [128, 128, 512], P(('prompt', 'comp'))
- d_w_uv: float32 [128, 512, 128], P(('prompt', 'comp'))
- d_latent: float32 [1024, 512], P(('prompt', 'comp'))
- d_rope_key: float32 [1024, 64], P(('prompt', 'comp'))
- d_comp_latent: float32 [2048, 512], P('comp', 'prompt')
- d_comp_rope: float32 [2048, 64], P('comp', 'prompt')
The draws below stay inside these ranges and needn't reach their ends.
All inputs are finite; a program needn't handle non-finite values.
Results may differ from the reference program's by a relative error of at most 0.012.
Values may be sent and summed in bfloat16 or wider, within the bound.
No kernel may reach another device: no remote copies, remote signals or barrier semaphores. Data moves between devices by JAX's collectives and lax.ppermute only.
A program may use at most 128 MiB of HBM per device.

```python
import jax
import jax.numpy as jnp
from jax import lax

HEADS = 128
D_LAT = 512
D_ROPE = 64
D_NOPE = 128
SLEN = 64
SAMPLES = 32
ROWS = 2048
PROMPT = 1024


def rope_base(key):
    return jnp.clip(jax.random.normal(key, (PROMPT, D_ROPE), jnp.float32), -4.0, 4.0)


def draw_rope_key(key, part):
    base = rope_base(key)
    return base.astype(jnp.bfloat16)


def draw_q_rope(key, part):
    key = jax.random.fold_in(key, 5)
    values = jnp.clip(jax.random.normal(key, (ROWS, HEADS, D_ROPE), jnp.float32), -4.0, 4.0)
    return values.reshape(ROWS, HEADS * D_ROPE).astype(jnp.bfloat16)


def place_ends(array, stream_key, smallest, top_value):
    place = [jax.random.randint(jax.random.fold_in(stream_key, axis), (), 0, length) for axis, length in enumerate(array.shape)]
    longest = array.shape.index(max(array.shape))
    neighbour = place[:longest] + [(place[longest] + 1) % array.shape[longest]] + place[longest + 1:]
    return array.at[tuple(place)].set(smallest).at[tuple(neighbour)].set(top_value)


def level_of(key, shape, pieces, smallest, top_value):
    def one(axis_at, shards_of):
        steps = jax.random.uniform(jax.random.fold_in(jax.random.fold_in(key, 6), axis_at), (shards_of,), jnp.float32, smallest / len(pieces), top_value / len(pieces))
        return jnp.repeat(jnp.exp(steps), shape[axis_at] // shards_of).reshape((-1,) + (1,) * (len(shape) - axis_at - 1))

    gain = one(*pieces[0])
    for cut in pieces[1:]:
        gain = gain * one(*cut)
    return gain


def centred(stream_key, shape, scale, reach, cuts=(), kind=jnp.bfloat16):
    values = jax.random.normal(stream_key, shape, jnp.float32) * scale
    if len(cuts) > 0:
        values = level_of(stream_key, shape, cuts, -0.22, 0.18) * values
    return jnp.clip(values, min=-reach, max=reach).astype(kind)


def setup_inputs(seed: int = 0) -> dict:
    arg_keys = jax.random.split(jax.random.key(seed), 11)
    q_nope = centred(arg_keys[0], (ROWS, HEADS * D_NOPE), 1.0, 6.0, ((0, 16), (1, 8)))
    q_rope = draw_q_rope(jax.random.fold_in(arg_keys[10], 71), 0)
    d_out = centred(arg_keys[2], (ROWS, HEADS * D_NOPE), 1.0, 6.0, ((0, 16), (1, 8)))
    w_uk = centred(arg_keys[3], (HEADS, D_NOPE, D_LAT), D_NOPE ** -0.5, 0.5, ((0, 8),))
    w_uv = centred(arg_keys[4], (HEADS, D_LAT, D_NOPE), D_LAT ** -0.5, 0.25, ((0, 8),))
    latent = centred(arg_keys[5], (PROMPT, D_LAT), 1.0, 6.0, ((0, 8),))
    rope_key = draw_rope_key(jax.random.fold_in(arg_keys[10], 71), 0)
    comp_latent = centred(arg_keys[7], (ROWS, D_LAT), 1.0, 6.0, ((0, 16),))
    comp_rope = centred(arg_keys[8], (ROWS, D_ROPE), 1.0, 6.0, ((0, 16),))
    lengths = place_ends(jax.random.randint(arg_keys[9], (SAMPLES,), 1, SLEN + 1), jax.random.fold_in(arg_keys[9], 1), 1, SLEN).astype(jnp.int32)
    return {"q_nope": q_nope, "q_rope": q_rope, "d_out": d_out, "w_uk": w_uk, "w_uv": w_uv, "latent": latent, "rope_key": rope_key, "comp_latent": comp_latent, "comp_rope": comp_rope, "lengths": lengths}


def reference(q_nope, q_rope, d_out, w_uk, w_uv, latent, rope_key, comp_latent, comp_rope, lengths):
    f32 = jnp.float32
    bf16 = jnp.bfloat16
    scale = 1.0 / (D_NOPE + D_ROPE) ** 0.5
    position = jnp.arange(ROWS, dtype=jnp.int32) % SLEN
    limit = jnp.repeat(lengths, SLEN)
    grads = jnp.where((position < limit)[:, None], d_out, jnp.zeros_like(d_out))
    qn_all = q_nope.reshape(ROWS, HEADS, D_NOPE).transpose(1, 0, 2)
    qr_all = q_rope.reshape(ROWS, HEADS, D_ROPE).transpose(1, 0, 2)
    g_all = grads.reshape(ROWS, HEADS, D_NOPE).transpose(1, 0, 2)
    lat = latent.astype(f32)
    rop = rope_key.astype(f32)
    clat = comp_latent.astype(f32).reshape(SAMPLES, SLEN, D_LAT)
    crop = comp_rope.astype(f32).reshape(SAMPLES, SLEN, D_ROPE)
    causal = jnp.arange(SLEN)[:, None] >= jnp.arange(SLEN)[None, :]

    def head_step(carry, xs):
        d_lat, d_rop, d_clat, d_crop = carry
        qn, qr, g, wk, wv = xs
        q_lat = jnp.dot(qn, wk, preferred_element_type=f32).astype(bf16)
        ql = q_lat.astype(f32)
        qrf = qr.astype(f32)
        ql_s = ql.reshape(SAMPLES, SLEN, D_LAT)
        qr_s = qrf.reshape(SAMPLES, SLEN, D_ROPE)
        sp = (jnp.einsum('rl,pl->rp', ql, lat) + jnp.einsum('rd,pd->rp', qrf, rop)) * scale
        ss = (jnp.einsum('stl,sul->stu', ql_s, clat) + jnp.einsum('std,sud->stu', qr_s, crop)) * scale
        ss = jnp.where(causal[None], ss, -jnp.inf)
        top = jnp.maximum(jnp.max(sp, axis=-1), jnp.max(ss, axis=-1).reshape(ROWS))
        ep = jnp.exp(sp - top[:, None])
        es = jnp.exp(ss - top.reshape(SAMPLES, SLEN)[..., None])
        total = jnp.sum(ep, axis=-1) + jnp.sum(es, axis=-1).reshape(ROWS)
        pp = ep / total[:, None]
        ps = es / total.reshape(SAMPLES, SLEN)[..., None]
        ppb = pp.astype(bf16).astype(f32)
        psb = ps.astype(bf16).astype(f32)
        o_lat = (jnp.einsum('rp,pl->rl', ppb, lat) + jnp.einsum('stu,sul->stl', psb, clat).reshape(ROWS, D_LAT)).astype(bf16)
        d_olat = jnp.einsum('rv,lv->rl', g.astype(f32), wv.astype(f32)).astype(bf16).astype(f32)
        do_s = d_olat.reshape(SAMPLES, SLEN, D_LAT)
        dpp = jnp.einsum('rl,pl->rp', d_olat, lat)
        dps = jnp.einsum('stl,sul->stu', do_s, clat)
        delta = jnp.sum(pp * dpp, axis=-1) + jnp.sum(ps * dps, axis=-1).reshape(ROWS)
        dsp = (scale * pp * (dpp - delta[:, None])).astype(bf16).astype(f32)
        dss = (scale * ps * (dps - delta.reshape(SAMPLES, SLEN)[..., None])).astype(bf16).astype(f32)
        d_qlat = (jnp.einsum('rp,pl->rl', dsp, lat) + jnp.einsum('stu,sul->stl', dss, clat).reshape(ROWS, D_LAT)).astype(bf16)
        d_lat = d_lat + jnp.einsum('rp,rl->pl', dsp, ql) + jnp.einsum('rp,rl->pl', ppb, d_olat)
        d_rop = d_rop + jnp.einsum('rp,rd->pd', dsp, qrf)
        d_clat = d_clat + (jnp.einsum('stu,stl->sul', dss, ql_s) + jnp.einsum('stu,stl->sul', psb, do_s)).reshape(ROWS, D_LAT)
        d_crop = d_crop + jnp.einsum('stu,std->sud', dss, qr_s).reshape(ROWS, D_ROPE)
        dwk = jnp.einsum('rn,rl->nl', qn.astype(f32), d_qlat.astype(f32))
        dwv = jnp.einsum('rl,rv->lv', o_lat.astype(f32), g.astype(f32))
        return (d_lat, d_rop, d_clat, d_crop), (dwk, dwv)

    init = (jnp.zeros((PROMPT, D_LAT), f32), jnp.zeros((PROMPT, D_ROPE), f32),
            jnp.zeros((ROWS, D_LAT), f32), jnp.zeros((ROWS, D_ROPE), f32))
    carry, stacked = lax.scan(head_step, init, (qn_all, qr_all, g_all, w_uk, w_uv))
    return stacked[0], stacked[1], carry[0], carry[1], carry[2], carry[3]
```

```python
import functools

import jax
import jax.numpy as jnp
from jax import lax
from jax.experimental import pallas as pl
from jax.experimental.pallas import tpu as pltpu
from jax.sharding import PartitionSpec as P

f32 = jnp.float32
bf16 = jnp.bfloat16
LOG2E = 1.4426950408889634

ROWS = 128
SLEN = 64
LAT = 512
ROPE = 64
NOPE = 128
KW = 640
HW = 384
PK = 1024
AK = PK + 2 * ROWS
SCALE = 1.0 / (NOPE + ROPE) ** 0.5


def nt(a, b):
    return lax.dot_general(a, b, (((1,), (1,)), ((), ())), preferred_element_type=f32)


def nn(a, b):
    return lax.dot_general(a, b, (((1,), (0,)), ((), ())), preferred_element_type=f32)


def prep_kernel(info, lens, qn, qr, do, lat, rope, clat, crop, keep, send, kv):
    core = info[0]
    row = lax.broadcasted_iota(jnp.int32, (ROWS, 1), 0)
    limit = jnp.where(row < SLEN, lens[0], lens[1])
    valid = (row % SLEN) < limit
    for out, flip in ((keep, 0), (send, 1)):
        par = core ^ flip
        for k in range(8):
            at = pl.multiple_of((2 * k + par) * NOPE, NOPE)
            out[k, :, 0:NOPE] = qn[:, pl.ds(at, NOPE)]
            g = do[:, pl.ds(at, NOPE)]
            out[k, :, NOPE : 2 * NOPE] = jnp.where(valid, g, jnp.zeros_like(g))
            pair = qr[:, 2 * ROPE * k : 2 * ROPE * (k + 1)].astype(f32)
            flipped = pltpu.roll(pair, ROPE, 1)
            out[k, :, 2 * NOPE : HW] = jnp.where(par == 0, pair, flipped).astype(bf16)
        out[8] = clat[:, 0:HW]
        out[9, :, 0 : LAT - HW] = clat[:, HW:LAT]
        out[9, :, LAT - HW : HW] = jnp.concatenate(
            [crop[...], jnp.zeros((ROWS, HW - (LAT - HW) - ROPE), bf16)], axis=1
        )
    mine = jnp.concatenate(
        [lat[...].astype(f32), rope[...].astype(f32), jnp.zeros((ROWS, KW - LAT - ROPE), f32)],
        axis=1,
    ).reshape(8, 2, 8, KW)
    kv[...] = jnp.where(core == 0, mine[:, 0], mine[:, 1]).reshape(64, KW).astype(bf16)


def prep(info, lens, qn, qr, do, lat, rope, clat, crop):
    vm = pl.BlockSpec(memory_space=pltpu.VMEM)
    sm = pl.BlockSpec(memory_space=pltpu.SMEM)
    return pl.pallas_call(
        prep_kernel,
        out_shape=(
            jax.ShapeDtypeStruct((10, ROWS, HW), bf16),
            jax.ShapeDtypeStruct((10, ROWS, HW), bf16),
            jax.ShapeDtypeStruct((64, KW), bf16),
        ),
        in_specs=[sm, sm] + [vm] * 7,
        out_specs=(vm, vm, vm),
        compiler_params=pltpu.CompilerParams(vmem_limit_bytes=24 * 2**20),
        name="prep",
    )(info, lens, qn, qr, do, lat, rope, clat, crop)


def attend_kernel(nh, first, last, info, *refs):
    refs = list(refs)
    take = lambda n: [refs.pop(0) for _ in range(n)]
    (kva, kvb, ckeep, crecv) = take(4)
    keeps, recvs, wks, wvs = take(nh), take(nh), take(nh), take(nh)
    accs = [] if first else take(1)
    dws = take(nh)
    outs = take(2) if last else take(1)
    (kall, kt, s_ref, dp_ref, pb, ds, q, dol) = refs
    W = 2 * ROWS
    kall[0:512] = kva[...]
    kall[512:1024] = kvb[...]
    for at, ref in ((PK, ckeep), (PK + ROWS, crecv)):
        kall[at : at + ROWS, 0:HW] = ref[0]
        kall[at : at + ROWS, HW:KW] = ref[1, :, 0 : KW - HW]
    for b in range(AK // 256):
        kt[:, b * 256 : b * 256 + 256] = kall[b * 256 : b * 256 + 256, 0:LAT].T
    zero = jnp.zeros((ROWS, ROWS), bf16)
    iu = lax.broadcasted_iota(jnp.int32, (ROWS, W), 0)
    it = lax.broadcasted_iota(jnp.int32, (ROWS, W), 1) % ROWS
    seen = ((iu // SLEN) == (it // SLEN)) & (iu <= it)
    NC = PK // 128 + 1
    for h in range(nh):
        lo = h * W
        hs = slice(lo, lo + W)
        qn = jnp.concatenate([keeps[h][0, :, 0:NOPE], recvs[h][0, :, 0:NOPE]], axis=0)
        g = jnp.concatenate(
            [keeps[h][0, :, NOPE : 2 * NOPE], recvs[h][0, :, NOPE : 2 * NOPE]], axis=0
        )
        q[hs, 0:LAT] = nn(qn, wks[h][0, 0]).astype(bf16)
        q[lo : lo + ROWS, LAT:KW] = keeps[h][0, :, 2 * NOPE : HW]
        q[lo + ROWS : lo + W, LAT:KW] = recvs[h][0, :, 2 * NOPE : HW]
        dol[hs] = nt(g, wvs[h][0, 0]).astype(bf16)
        sv, dv = s_ref.at[h % 2], dp_ref.at[h % 2]
        sv[0:PK] = nt(kall[0:PK], q[hs])
        own = nt(kall[PK:AK], q[hs])
        own = jnp.concatenate([own[0:ROWS, 0:ROWS], own[ROWS:W, ROWS:W]], axis=1)
        sv[PK : PK + ROWS] = jnp.where(seen, own, -jnp.inf)
        dv[0:PK] = nt(kall[0:PK, 0:LAT], dol[hs])
        own = nt(kall[PK:AK, 0:LAT], dol[hs])
        dv[PK : PK + ROWS] = jnp.concatenate(
            [own[0:ROWS, 0:ROWS], own[ROWS:W, ROWS:W]], axis=1
        )
        top = jnp.full((8, W), -jnp.inf, f32)
        for c in range(NC):
            x = sv[c * 128 : c * 128 + 128].reshape(16, 8, W)
            top = jnp.maximum(top, jnp.max(x, axis=0))
        top = jnp.max(top, axis=0, keepdims=True)
        total = jnp.zeros((8, W), f32)
        delta = jnp.zeros((8, W), f32)
        for c in range(NC):
            cs = slice(c * 128, c * 128 + 128)
            e = jnp.exp2((sv[cs] - top) * (SCALE * LOG2E))
            sv[cs] = e
            total = total + jnp.sum(e.reshape(16, 8, W), axis=0)
            delta = delta + jnp.sum((e * dv[cs]).reshape(16, 8, W), axis=0)
        inv = 1.0 / jnp.sum(total, axis=0, keepdims=True)
        delta = jnp.sum(delta, axis=0, keepdims=True) * inv
        cinv = inv * SCALE
        for c in range(NC):
            cs = slice(c * 128, c * 128 + 128)
            e = sv[cs]
            p = (e * inv).astype(bf16)
            d = (e * cinv * (dv[cs] - delta)).astype(bf16)
            if c < NC - 1:
                pb[cs, hs] = p
                ds[cs, hs] = d
            else:
                for ref, x in ((pb, p), (ds, d)):
                    ref[PK : PK + ROWS, lo : lo + ROWS] = x[:, 0:ROWS]
                    ref[PK : PK + ROWS, lo + ROWS : lo + W] = zero
                    ref[PK + ROWS : AK, lo : lo + ROWS] = zero
                    ref[PK + ROWS : AK, lo + ROWS : lo + W] = x[:, ROWS:W]
        olat_t = nn(kt[...], pb[:, hs]).astype(bf16)
        dqlat_t = nn(kt[...], ds[:, hs]).astype(bf16)
        dwk = nt(qn.T, dqlat_t)
        for j in range(4):
            dws[h][j * 128 : j * 128 + 128] = dwk[:, j * 128 : j * 128 + 128].astype(bf16)
        dws[h][LAT : 2 * LAT] = nn(olat_t, g).astype(bf16)
    if last:
        stay, give = outs
    for b in range(AK // 128):
        bs = slice(b * 128, b * 128 + 128)
        r = nn(ds[bs], q[...])
        r = jnp.concatenate([r[:, 0:LAT] + nn(pb[bs], dol[...]), r[:, LAT:KW]], axis=1)
        if not first:
            r = r + accs[0][bs]
        if not last:
            outs[0][bs] = r
        elif b < 4:
            stay[bs] = r.astype(bf16)
        elif b < 8:
            give[(b - 4) * 128 : (b - 4) * 128 + 128] = r.astype(bf16)
        elif b == 8:
            stay[512:640] = r.astype(bf16)
        else:
            give[512:640] = r.astype(bf16)


def attend(nh, first, last, info, kva, kvb, keep, recv, w_uk, w_uv, acc):
    W = 2 * ROWS
    vm = pl.BlockSpec(memory_space=pltpu.VMEM)

    def head(i):
        return pl.BlockSpec((1, ROWS, HW), lambda s, info: (info[i + 1], 0, 0))

    ck = pl.BlockSpec((2, ROWS, HW), lambda s, info: (4, 0, 0))

    def wspec(i, a, b):
        return pl.BlockSpec((1, 1, a, b), lambda s, info: (info[i + 1], info[0], 0, 0))

    def full(a, b):
        return pl.BlockSpec((a, b), lambda s, info: (0, 0))

    in_specs = [full(512, KW), full(512, KW), ck, ck]
    in_specs += [head(i) for i in range(nh)] * 2
    in_specs += [wspec(i, NOPE, LAT) for i in range(nh)]
    in_specs += [wspec(i, LAT, NOPE) for i in range(nh)]
    ops = [kva, kvb, keep, recv] + [keep] * nh + [recv] * nh + [w_uk] * nh + [w_uv] * nh
    if not first:
        in_specs.append(full(AK, KW))
        ops.append(acc)
    out_specs = [full(2 * LAT, NOPE)] * nh
    out_shape = [jax.ShapeDtypeStruct((2 * LAT, NOPE), bf16)] * nh
    if last:
        out_specs += [full(640, KW)] * 2
        out_shape += [jax.ShapeDtypeStruct((640, KW), bf16)] * 2
    else:
        out_specs += [full(AK, KW)]
        out_shape += [jax.ShapeDtypeStruct((AK, KW), f32)]
    return pl.pallas_call(
        functools.partial(attend_kernel, nh, first, last),
        out_shape=out_shape,
        grid_spec=pltpu.PrefetchScalarGridSpec(
            num_scalar_prefetch=1,
            grid=(1,),
            in_specs=in_specs,
            out_specs=out_specs,
            scratch_shapes=[
                pltpu.VMEM((AK, KW), bf16),
                pltpu.VMEM((LAT, AK), bf16),
                pltpu.VMEM((2, PK + ROWS, W), f32),
                pltpu.VMEM((2, PK + ROWS, W), f32),
                pltpu.VMEM((AK, nh * W), bf16),
                pltpu.VMEM((AK, nh * W), bf16),
                pltpu.VMEM((nh * W, KW), bf16),
                pltpu.VMEM((nh * W, LAT), bf16),
            ],
        ),
        compiler_params=pltpu.CompilerParams(vmem_limit_bytes=50 * 2**20),
        name="attend",
    )(info, *ops)


def join_kernel(info, stay, got, dlat, dcl):
    prm = info[0]
    for k in range(8):
        to = lax.rem(prm - k + 8, 8)
        at = pl.multiple_of(to * 64, 64)
        ks = slice(k * 64, k * 64 + 64)
        dlat[pl.ds(at, 64)] = (stay[ks].astype(f32) + got[ks].astype(f32)).astype(bf16)
    c = stay[512:640].astype(f32) + got[512:640].astype(f32)
    pad = jnp.zeros((ROWS, 56), f32)
    for j in range(8):
        dcl[j] = jnp.concatenate(
            [c[:, 64 * j : 64 * j + 64], c[:, LAT + 8 * j : LAT + 8 * j + 8], pad], axis=1
        ).astype(bf16)


def join(info, stay, got):
    vm = pl.BlockSpec(memory_space=pltpu.VMEM)
    return pl.pallas_call(
        join_kernel,
        out_shape=(
            jax.ShapeDtypeStruct((512, KW), bf16),
            jax.ShapeDtypeStruct((8, ROWS, 128), bf16),
        ),
        in_specs=[pl.BlockSpec(memory_space=pltpu.SMEM), vm, vm],
        out_specs=(vm, vm),
        compiler_params=pltpu.CompilerParams(vmem_limit_bytes=24 * 2**20),
        name="join",
    )(info, stay, got)


def weights_kernel(*refs):
    parts, (dwk, dwv) = refs[:-2], refs[-2:]
    for j in range(4):
        js = slice(j * 128, j * 128 + 128)
        total = parts[0][js].astype(f32)
        for p in parts[1:]:
            total = total + p[js].astype(f32)
        dwk[:, js] = total
        js = slice(LAT + j * 128, LAT + j * 128 + 128)
        total = parts[0][js].astype(f32)
        for p in parts[1:]:
            total = total + p[js].astype(f32)
        dwv[j * 128 : j * 128 + 128] = total


def weights(parts):
    vm = pl.BlockSpec(memory_space=pltpu.VMEM)
    return pl.pallas_call(
        weights_kernel,
        out_shape=(
            jax.ShapeDtypeStruct((NOPE, LAT), f32),
            jax.ShapeDtypeStruct((LAT, NOPE), f32),
        ),
        in_specs=[vm] * len(parts),
        out_specs=(vm, vm),
        compiler_params=pltpu.CompilerParams(vmem_limit_bytes=24 * 2**20),
        name="weights",
    )(*parts)


def final_kernel(info, dcl, *refs):
    got, dlat, (ol, orp, ocl, ocr) = refs[:7], refs[7], refs[8:]
    total = dcl[info[0]].astype(f32)
    for p in got:
        total = total + p[...].astype(f32)
    ocl[...] = total[:, 0:64]
    ocr[...] = total[:, 64:72]
    x = jnp.sum(dlat[...].astype(f32).reshape(64, 8, KW), axis=0)
    ol[...] = x[:, 0:LAT]
    orp[...] = x[:, LAT : LAT + ROPE]


def final(info, dcl, got, dlat):
    vm = pl.BlockSpec(memory_space=pltpu.VMEM)
    return pl.pallas_call(
        final_kernel,
        out_shape=(
            jax.ShapeDtypeStruct((8, LAT), f32),
            jax.ShapeDtypeStruct((8, ROPE), f32),
            jax.ShapeDtypeStruct((ROWS, 64), f32),
            jax.ShapeDtypeStruct((ROWS, 8), f32),
        ),
        in_specs=[pl.BlockSpec(memory_space=pltpu.SMEM)] + [vm] * 9,
        out_specs=(vm,) * 4,
        compiler_params=pltpu.CompilerParams(vmem_limit_bytes=24 * 2**20),
        name="final",
    )(info, dcl, *got, dlat)


NH = 4
HOPS = ((2, 1), (2, 0), (1, 1), (1, 0), (3, 1), (3, 0), (0, 1), (0, 0))


def chip_perm(dz, dx):
    return [
        (c, (((c >> 2) + dz) % 4) * 4 + ((((c >> 1) & 1) ^ dx) << 1) + (c & 1))
        for c in range(16)
    ]


def local(q_nope, q_rope, d_out, w_uk, w_uv, latent, rope_key, comp_latent, comp_rope, lengths):
    comp = lax.axis_index("comp").astype(jnp.int32)
    prm = lax.axis_index("prompt").astype(jnp.int32)
    core, z, xh = comp % 2, comp // 4, (comp // 2) % 2
    core_perm = [(c, c ^ 1) for c in range(16)]
    keep, send, kv = prep(
        core[None], lengths, q_nope, q_rope, d_out, latent, rope_key, comp_latent, comp_rope
    )
    parts = [kv] + [
        lax.ppermute(kv, "prompt", [(i, (i + k) % 8) for i in range(8)]) for k in range(1, 8)
    ]
    recv = lax.ppermute(send, "comp", core_perm)
    kva = jnp.concatenate(parts, axis=0)
    kvb = lax.ppermute(kva, "comp", core_perm)
    w_uk4 = w_uk.reshape(8, 2, NOPE, LAT)
    w_uv4 = w_uv.reshape(8, 2, LAT, NOPE)
    order = [((z + dz) % 4) * 2 + (xh ^ dx) for dz, dx in HOPS]
    acc = None
    sums = []
    for first in range(0, 8, NH):
        info = jnp.stack([core] + order[first : first + NH])
        done = first + NH == 8
        out = attend(
            NH, first == 0, done, info, kva, kvb, keep, recv, w_uk4, w_uv4, acc
        )
        acc = out[NH]
        for i in range(NH):
            hop = HOPS[first + i]
            if hop == (0, 0):
                sums.append(out[i])
            else:
                sums.append(lax.ppermute(out[i], "comp", chip_perm(*hop)))
    stay, give = out[NH], out[NH + 1]
    got = lax.ppermute(give, "comp", core_perm)
    dlat, dcl = join(prm[None], stay, got)
    pieces = [
        lax.ppermute(
            lax.dynamic_index_in_dim(dcl, (prm + k) % 8, 0, keepdims=False),
            "prompt",
            [(i, (i + k) % 8) for i in range(8)],
        )
        for k in range(1, 8)
    ]
    groups = [[i for i in range(128) if i % 2 == c] for c in range(2)]
    dlat = lax.all_to_all(
        dlat, ("prompt", "comp"), 0, 0, tiled=True, axis_index_groups=groups
    )
    dwk, dwv = weights(sums)
    ol, orp, ocl, ocr = final(prm[None], dcl, pieces, dlat)
    return dwk[None], dwv[None], ol, orp, ocl, ocr


def solution(mesh):
    in_specs = (
        P("comp", "prompt"),
        P("comp", "prompt"),
        P("comp", "prompt"),
        P("prompt", None, None),
        P("prompt", None, None),
        P("prompt", None),
        P("prompt", None),
        P("comp", None),
        P("comp", None),
        P("comp"),
    )
    out_specs = (
        P(("prompt", "comp"), None, None),
        P(("prompt", "comp"), None, None),
        P(("prompt", "comp"), None),
        P(("prompt", "comp"), None),
        P("comp", "prompt"),
        P("comp", "prompt"),
    )
    return jax.shard_map(local, mesh=mesh, in_specs=in_specs, out_specs=out_specs, check_vma=False)
```

```python
import functools

import jax
import jax.numpy as jnp
from jax import lax
from jax.experimental import pallas as pl
from jax.experimental.pallas import tpu as pltpu
from jax.sharding import PartitionSpec as P

f32 = jnp.float32
bf16 = jnp.bfloat16
LOG2E = 1.4426950408889634

ROWS = 128
SLEN = 64
LAT = 512
ROPE = 64
NOPE = 128
KW = 640
HW = 384
W = 2 * ROWS
PK = 1024
AK = PK + 2 * ROWS
SCALE = 1.0 / (NOPE + ROPE) ** 0.5


def nt(a, b):
    return lax.dot_general(a, b, (((1,), (1,)), ((), ())), preferred_element_type=f32)


def nn(a, b):
    return lax.dot_general(a, b, (((1,), (0,)), ((), ())), preferred_element_type=f32)


def params(mib=60):
    return pltpu.CompilerParams(vmem_limit_bytes=mib * 2**20)


def cost(flops, nbytes):
    return pl.CostEstimate(flops=flops, bytes_accessed=nbytes, transcendentals=0)


VM = pl.BlockSpec(memory_space=pltpu.VMEM)
SM = pl.BlockSpec(memory_space=pltpu.SMEM)


def keys_kernel(lat, rope_t, kv):
    core = lax.axis_index("comp") % 2
    x = jnp.concatenate(
        [lat[...].astype(f32), rope_t[...].astype(f32).T, jnp.zeros((ROWS, KW - LAT - ROPE), f32)],
        axis=1,
    ).reshape(8, 2, 8, KW)
    x = jnp.where(core == 0, x[:, 0], x[:, 1]).reshape(64, KW).astype(bf16)
    for k in range(8):
        kv[k] = x


def keys(lat, rope_t):
    return pl.pallas_call(
        keys_kernel,
        out_shape=jax.ShapeDtypeStruct((8, 64, KW), bf16),
        in_specs=[VM, VM],
        out_specs=VM,
        compiler_params=params(),
        name="keys",
    )(lat, rope_t)


def prep_kernel(info, lens, *refs):
    core = info[0]
    row = lax.broadcasted_iota(jnp.int32, (ROWS, 1), 0)
    limit = jnp.where(row < SLEN, lens[0], lens[1])
    valid = (row % SLEN) < limit
    lane = lax.broadcasted_iota(jnp.int32, (ROWS, 2 * ROPE), 1)
    keep, send, ww = refs[-3:]
    for h in range(2):
        qn_k, qn_s, do_k, do_s, qr, wk, wv = refs[7 * h : 7 * h + 7]
        tile = qr[...].astype(f32)
        flipped = pltpu.roll(tile, ROPE, 1)
        for out, qn, do, par in ((keep, qn_k, do_k, core), (send, qn_s, do_s, 1 - core)):
            out[h, :, 0:NOPE] = qn[...]
            x = jnp.where(lane < ROPE, jnp.where(par == 0, tile, flipped), 0.0)
            out[h, :, NOPE : 2 * NOPE] = x.astype(bf16)
            g = do[...]
            out[h, :, 2 * NOPE : HW] = jnp.where(valid, g, jnp.zeros_like(g))
        ww[h, 0:NOPE] = wk[0]
        ww[h, NOPE : 2 * NOPE] = wv[0].T


def own_kernel(clat, crop_t, after, out):
    out[:, 0:LAT] = clat[...]
    pad = jnp.zeros((ROWS, KW - LAT - ROPE), bf16)
    crop = crop_t[...].astype(f32).T.astype(bf16)
    out[:, LAT:KW] = jnp.concatenate([crop, pad], axis=1)


def own_keys(clat, crop_t, after):
    return pl.pallas_call(
        own_kernel,
        out_shape=jax.ShapeDtypeStruct((ROWS, KW), bf16),
        in_specs=[VM, VM, pl.BlockSpec(memory_space=pl.ANY)],
        out_specs=VM,
        compiler_params=params(4),
        cost_estimate=cost(3 * 10**9, 4 * 2**20),
        name="own_keys",
    )(clat, crop_t, after)


def prep(info, lens, qn, qr, do, w_uk, w_uv):
    def head(i, info, flip):
        core = info[0]
        return 2 * info[5 + i] + (1 - core if flip else core)

    in_specs, ops = [], []
    for h in range(2):

        def cols(flip, h=h):
            return pl.BlockSpec((ROWS, NOPE), lambda i, info, lens: (0, head(2 * i + h, info, flip)))

        def weight(a, b, h=h):
            return pl.BlockSpec(
                (1, a, b), lambda i, info, lens: (head(2 * i + h, info, False), 0, 0)
            )

        def pair(h=h):
            return pl.BlockSpec((ROWS, 2 * ROPE), lambda i, info, lens: (0, info[5 + 2 * i + h]))

        in_specs += [cols(False), cols(True), cols(False), cols(True), pair()]
        in_specs += [weight(NOPE, LAT), weight(LAT, NOPE)]
        ops += [qn, qn, do, do, qr, w_uk, w_uv]
    out = pl.BlockSpec((2, ROWS, HW), lambda i, info, lens: (i, 0, 0))
    return pl.pallas_call(
        prep_kernel,
        out_shape=(
            jax.ShapeDtypeStruct((8, ROWS, HW), bf16),
            jax.ShapeDtypeStruct((8, ROWS, HW), bf16),
            jax.ShapeDtypeStruct((8, 2 * NOPE, LAT), bf16),
        ),
        grid_spec=pltpu.PrefetchScalarGridSpec(
            num_scalar_prefetch=2,
            grid=(4,),
            in_specs=in_specs,
            out_specs=(
                out,
                out,
                pl.BlockSpec((2, 2 * NOPE, LAT), lambda i, info, lens: (i, 0, 0)),
            ),
        ),
        compiler_params=params(),
        cost_estimate=cost(10**9, 4 * 2**20),
        name="prep",
    )(info, lens, *ops)


HPS = 2
STEPS = 2


def attend_kernel(last, *refs):
    refs = list(refs)

    def take(n):
        return [refs.pop(0) for _ in range(n)]

    kva, kvb, ckeep, crecv, keep, recv, ww = take(7)
    if last:
        (acc,) = take(1)
        rest, stay, give_a, give_b, give_c = take(5)
    else:
        plus, minus, acc = take(3)
    kall, kt, kx, s_ref, dp_ref, pb, ds, xy, rop = take(9)
    step = pl.program_id(0)
    CH = 128
    NC = (PK + ROWS) // CH

    @pl.when(step == 0)
    def _():
        for at, ref in ((0, kva), (512, kvb)):
            kall[at : at + 512] = ref[:, 0:LAT]
            for h in range(HPS):
                kx[h, at : at + 512, 128:256] = ref[:, LAT:KW]
        for at, ref in ((PK, ckeep), (PK + ROWS, crecv)):
            kall[at : at + ROWS] = ref[:, 0:LAT]
            for h in range(HPS):
                kx[h, at : at + ROWS, 128:256] = ref[:, LAT:KW]
        for b in range(AK // 256):
            kt[:, b * 256 : b * 256 + 256] = kall[b * 256 : b * 256 + 256, :].T
        zero = jnp.zeros((ROWS, ROWS), bf16)
        for ref in (pb, ds):
            for h in range(HPS):
                ref[h, PK : PK + ROWS, ROWS:W] = zero
                ref[h, PK + ROWS : AK, 0:ROWS] = zero
        rop[...] = acc[:, LAT:KW] if last else jnp.zeros_like(rop)

    iu = lax.broadcasted_iota(jnp.int32, (ROWS, W), 0)
    it = lax.broadcasted_iota(jnp.int32, (ROWS, W), 1) % ROWS
    seen = ((iu // SLEN) == (it // SLEN)) & (iu <= it)
    queries = []
    for h in range(HPS):
        at = pl.multiple_of((step * HPS + h) * W, W)
        r = nt(kall[...], ww[pl.ds(at, W), :])
        kx[h, :, 0:128] = r[:, 0:128].astype(bf16)
        kx[h, :, 256:384] = r[:, 128:256].astype(bf16)
    for h in range(HPS):
        qx = jnp.concatenate([keep[h, :, 0:256], recv[h, :, 0:256]], axis=0)
        g = jnp.concatenate([keep[h, :, 256:HW], recv[h, :, 256:HW]], axis=0)
        queries.append((qx, g))
        s_ref[h, 0:PK] = nt(kx[h, 0:PK, 0:256], qx)
        own = nt(kx[h, PK:AK, 0:256], qx)
        own = jnp.concatenate([own[0:ROWS, 0:ROWS], own[ROWS:W, ROWS:W]], axis=1)
        s_ref[h, PK : PK + ROWS] = jnp.where(seen, own, -jnp.inf)
        dp_ref[h, 0:PK] = nt(kx[h, 0:PK, 256:384], g)
        own = nt(kx[h, PK:AK, 256:384], g)
        dp_ref[h, PK : PK + ROWS] = jnp.concatenate(
            [own[0:ROWS, 0:ROWS], own[ROWS:W, ROWS:W]], axis=1
        )
    both = []
    for h in range(HPS):
        qx, g = queries[h]
        top = jnp.full((8, W), -jnp.inf, f32)
        for c in range(NC):
            x = s_ref[h, c * CH : c * CH + CH].reshape(CH // 8, 8, W)
            top = jnp.maximum(top, jnp.max(x, axis=0))
        top = jnp.max(top, axis=0, keepdims=True)
        total = jnp.zeros((8, W), f32)
        delta = jnp.zeros((8, W), f32)
        for c in range(NC):
            cs = slice(c * CH, c * CH + CH)
            e = jnp.exp2((s_ref[h, cs] - top) * (SCALE * LOG2E))
            s_ref[h, cs] = e
            total = total + jnp.sum(e.reshape(CH // 8, 8, W), axis=0)
            delta = delta + jnp.sum((e * dp_ref[h, cs]).reshape(CH // 8, 8, W), axis=0)
        inv = 1.0 / jnp.sum(total, axis=0, keepdims=True)
        delta = jnp.sum(delta, axis=0, keepdims=True) * inv
        cinv = inv * SCALE
        for c in range(NC):
            cs = slice(c * CH, c * CH + CH)
            e = s_ref[h, cs]
            p = (e * inv).astype(bf16)
            d = (e * cinv * (dp_ref[h, cs] - delta)).astype(bf16)
            if c < NC - 1:
                pb[h, cs] = p
                ds[h, cs] = d
            else:
                for ref, x in ((pb, p), (ds, d)):
                    ref[h, PK : PK + ROWS, 0:ROWS] = x[:, 0:ROWS]
                    ref[h, PK + ROWS : AK, ROWS:W] = x[:, ROWS:W]
        x = nn(ds[h], qx)
        rop[...] += x[:, 128:256]
        y = nn(pb[h], g)
        xx = jnp.concatenate([x[:, 0:128].astype(bf16), y.astype(bf16)], axis=1)
        at = pl.multiple_of((step * HPS + h) * W, W)
        xy[:, pl.ds(at, W)] = xx
        both.append(xx)
    for h in range(HPS):
        out = nn(kt[...], both[h]).astype(bf16)
        if last:
            rest[h] = out
        elif h == 0:
            plus[0] = out
        else:
            minus[0] = out

    @pl.when(step == STEPS - 1)
    def _():
        r = nn(xy[...], ww[...])
        if last:
            r = jnp.concatenate([r + acc[:, 0:LAT], rop[...]], axis=1).astype(bf16)
            stay[0:512] = r[0:512]
            stay[512:640] = r[PK : PK + ROWS]
            give_a[...] = r[512:768]
            give_b[...] = r[768:1024]
            give_c[...] = r[PK + ROWS : AK]
        else:
            acc[:, 0:LAT] = r
            acc[:, LAT:KW] = rop[...]


def attend(last, kva, kvb, ckeep, crecv, keep, recv, ww, acc=None):
    base = 2 if last else 0

    def full(a, b):
        return pl.BlockSpec((a, b), lambda s: (0, 0))

    def block(n):
        return pl.BlockSpec((n, LAT, 2 * NOPE), lambda s: (s, 0, 0))

    def shape(n):
        return jax.ShapeDtypeStruct((n, LAT, 2 * NOPE), bf16)

    heads = pl.BlockSpec((HPS, ROWS, HW), lambda s: (base + s, 0, 0))
    ckeys = full(ROWS, KW)
    weights = pl.BlockSpec((STEPS * HPS * W, LAT), lambda s: (base // 2, 0))
    in_specs = [full(512, KW), full(512, KW), ckeys, ckeys, heads, heads, weights]
    ops = [kva, kvb, ckeep, crecv, keep, recv, ww]
    scratch = [
        pltpu.VMEM((AK, LAT), bf16),
        pltpu.VMEM((LAT, AK), bf16),
        pltpu.VMEM((HPS, AK, 384), bf16),
        pltpu.VMEM((HPS, PK + ROWS, W), f32),
        pltpu.VMEM((HPS, PK + ROWS, W), f32),
        pltpu.VMEM((HPS, AK, W), bf16),
        pltpu.VMEM((HPS, AK, W), bf16),
        pltpu.VMEM((AK, STEPS * HPS * W), bf16),
        pltpu.VMEM((AK, 128), f32),
    ]
    if last:
        in_specs.append(full(AK, KW))
        ops.append(acc)
        out_shape = [shape(4)]
        out_specs = [block(2)]
        for n in (640, 256, 256, ROWS):
            out_shape.append(jax.ShapeDtypeStruct((n, KW), bf16))
            out_specs.append(full(n, KW))
    else:
        out_shape = (shape(2), shape(2), jax.ShapeDtypeStruct((AK, KW), f32))
        out_specs = (block(1), block(1), full(AK, KW))
    return pl.pallas_call(
        functools.partial(attend_kernel, last),
        out_shape=out_shape,
        grid=(STEPS,),
        in_specs=in_specs,
        out_specs=out_specs,
        scratch_shapes=scratch,
        compiler_params=params(36),
        cost_estimate=cost(10**10, 10 * 2**20),
        name="attend",
    )(*ops)


YW = 768


def join_kernel(info, stay, got_a, got_b, got_c, o0, o1, o2, o3):
    y = info[1]
    crope = stay[512:640, LAT:KW].astype(f32) + got_c[:, LAT:KW].astype(f32)
    for k, out in enumerate((o0, o1, o2, o3)):
        to = lax.rem(y + k, 4)
        at = pl.multiple_of(to * 128, 128)
        row = pl.ds(at, 128)
        half = pl.ds(pl.multiple_of(lax.rem(to, 2) * 128, 128), 128)
        got = jnp.where(to < 2, got_a[half, :].astype(f32), got_b[half, :].astype(f32))
        x = stay[row, :].astype(f32) + got
        c = stay[512:640, row].astype(f32) + got_c[:, row].astype(f32)
        r = pltpu.roll(crope, lax.rem(KW - LAT + ROPE - 16 * to, KW - LAT), 1)
        lane = lax.broadcasted_iota(jnp.int32, (ROWS, KW - LAT), 1)
        tail = jnp.where(lane < ROPE, x[:, LAT:KW], r)
        out[:, 0:LAT] = x[:, 0:LAT].astype(bf16)
        out[:, LAT:KW] = tail.astype(bf16)
        out[:, KW:YW] = c.astype(bf16)


def join(info, stay, *got):
    return pl.pallas_call(
        join_kernel,
        out_shape=(jax.ShapeDtypeStruct((128, YW), bf16),) * 4,
        in_specs=[SM] + [VM] * 4,
        out_specs=(VM,) * 4,
        compiler_params=params(24),
        name="join",
    )(info, stay, *got)


def sum_y_kernel(info, a0, a1, a2, a3, out, mine, send):
    xl = info[2]
    x = a0[...].astype(f32) + a1[...].astype(f32) + a2[...].astype(f32) + a3[...].astype(f32)
    out[...] = x[:, 0:KW].astype(bf16)
    lane = lax.broadcasted_iota(jnp.int32, (ROWS, 128), 1)
    lat, rope = x[:, KW:YW], x[:, LAT:KW]
    for ref, flip in ((mine, 0), (send, 1)):
        to = xl ^ flip
        c = pltpu.roll(lat, lax.rem(128 - 64 * to, 128), 1)
        r = pltpu.roll(rope, lax.rem(128 - 8 * to, 128), 1)
        ref[...] = jnp.where(lane < 64, c, r).astype(bf16)


def sum_y(info, *parts):
    return pl.pallas_call(
        sum_y_kernel,
        out_shape=(
            jax.ShapeDtypeStruct((128, KW), bf16),
            jax.ShapeDtypeStruct((ROWS, 128), bf16),
            jax.ShapeDtypeStruct((ROWS, 128), bf16),
        ),
        in_specs=[SM] + [VM] * 4,
        out_specs=(VM,) * 3,
        compiler_params=params(24),
        name="sum_y",
    )(info, *parts)


def final_kernel(mine, got, dlat, after, ol, orp, ocl, ocr):
    c = (mine[...].astype(f32) + got[...].astype(f32)).T
    ocl[...] = c[0:64]
    ocr[...] = c[64:72]
    x = jnp.sum(dlat[...].astype(f32).reshape(16, 8, KW), axis=0)
    ol[...] = x[:, 0:LAT]
    orp[...] = x[:, LAT : LAT + ROPE]


def final(mine, got, dlat, after):
    return pl.pallas_call(
        final_kernel,
        out_shape=(
            jax.ShapeDtypeStruct((8, LAT), f32),
            jax.ShapeDtypeStruct((8, ROPE), f32),
            jax.ShapeDtypeStruct((64, ROWS), f32),
            jax.ShapeDtypeStruct((8, ROWS), f32),
        ),
        in_specs=[VM] * 4,
        out_specs=(VM,) * 4,
        compiler_params=params(24),
        name="final",
    )(mine, got, dlat, after)


def ring_kernel(rest, p, m, after, a, b):
    a[...] = (rest[0].astype(f32) + p[0].astype(f32)).astype(bf16)
    b[...] = (rest[1].astype(f32) + m[0].astype(f32)).astype(bf16)


def ring(rest, p, m, after):
    block = jax.ShapeDtypeStruct((LAT, 2 * NOPE), bf16)
    return pl.pallas_call(
        ring_kernel,
        out_shape=(block, block),
        in_specs=[VM] * 3 + [pl.BlockSpec(memory_space=pl.ANY)],
        out_specs=(VM, VM),
        compiler_params=params(24),
        name="ring",
    )(rest, p, m, after)


def pair_kernel(info, rest, p, m, a, b, mine, send):
    first = rest[2].astype(f32) + m[1].astype(f32) + a[...].astype(f32)
    second = rest[3].astype(f32) + p[1].astype(f32) + b[...].astype(f32)
    own = info[3] == 0
    mine[...] = jnp.where(own, first, second).astype(bf16)
    send[...] = jnp.where(own, second, first).astype(bf16)


def pair(info, rest, p, m, a, b):
    block = jax.ShapeDtypeStruct((LAT, 2 * NOPE), bf16)
    return pl.pallas_call(
        pair_kernel,
        out_shape=(block, block),
        in_specs=[SM] + [VM] * 5,
        out_specs=(VM, VM),
        compiler_params=params(24),
        name="pair",
    )(info, rest, p, m, a, b)


def weights_kernel(mine, got, dwk, dwv, done):
    done[...] = jnp.zeros_like(done)
    x = mine[...].astype(f32) + got[...].astype(f32)
    dwk[...] = x[:, 0:NOPE].T
    dwv[...] = x[:, NOPE : 2 * NOPE]


def weights(mine, got):
    return pl.pallas_call(
        weights_kernel,
        out_shape=(
            jax.ShapeDtypeStruct((NOPE, LAT), f32),
            jax.ShapeDtypeStruct((LAT, NOPE), f32),
            jax.ShapeDtypeStruct((8, 128), f32),
        ),
        in_specs=[VM, VM],
        out_specs=(VM, VM, VM),
        compiler_params=params(24),
        name="weights",
    )(mine, got)


def local(q_nope, q_rope, d_out, w_uk, w_uv, latent, rope_key, comp_latent, comp_rope, lengths):
    comp = lax.axis_index("comp").astype(jnp.int32)
    prm = lax.axis_index("prompt").astype(jnp.int32)
    z = comp // 4
    far, after, before = (z + 2) % 4, (z + 1) % 4, (z + 3) % 4
    info = jnp.stack(
        [comp % 2, prm // 2, prm % 2, (comp // 2) % 2, z]
        + [2 * far, 2 * far + 1, 2 * after + 1, 2 * before]
        + [2 * after, 2 * before + 1, 2 * z, 2 * z + 1]
    )
    swap = [(c, c ^ 1) for c in range(16)]
    up = [(c, (c + 4) % 16) for c in range(16)]
    down = [(c, (c + 12) % 16) for c in range(16)]
    kv = keys(latent, rope_key.T)
    kva = lax.all_to_all(kv, "prompt", 0, 0, tiled=True).reshape(512, KW)
    keep, send, ww = prep(
        info, lengths, q_nope, q_rope, d_out, w_uk, w_uv
    )
    recv = lax.ppermute(send, "comp", swap)
    ckeep = own_keys(comp_latent, comp_rope.T, ww)
    crecv = lax.ppermute(ckeep, "comp", swap)
    kvb = lax.ppermute(kva, "comp", swap)
    ops = (kva, kvb, ckeep, crecv, keep, recv, ww.reshape(8 * W, LAT))
    plus, minus, acc = attend(False, *ops)
    plus = lax.ppermute(plus, "comp", up)
    minus = lax.ppermute(minus, "comp", down)
    rest, stay, *give = attend(True, *ops, acc)
    got = [lax.ppermute(x, "comp", swap) for x in give]
    o = join(info, stay, *got)
    o = [o[0]] + [
        lax.ppermute(o[k], "prompt", [(i, (i + 2 * k) % 8) for i in range(8)]) for k in (1, 2, 3)
    ]
    a, b = ring(rest, plus, minus, o[0])
    a = lax.ppermute(a, "comp", up)
    b = lax.ppermute(b, "comp", down)
    dlat, cmine, csend = sum_y(info, *o)
    planes = [
        [(2 * y + xl) * 16 + 2 * i + core for xl in range(2) for i in range(8)]
        for y in range(4)
        for core in range(2)
    ]
    cgot = lax.ppermute(csend, "prompt", [(i, i ^ 1) for i in range(8)])
    dlat = lax.all_to_all(
        dlat, ("prompt", "comp"), 0, 0, tiled=True, axis_index_groups=planes
    )
    mine, send = pair(info, rest, plus, minus, a, b)
    other = lax.ppermute(send, "comp", [(c, c ^ 2) for c in range(16)])
    dwk, dwv, done = weights(mine, other)
    ol, orp, ocl, ocr = final(cmine, cgot, dlat, done)
    return dwk[None], dwv[None], ol, orp, ocl.T, ocr.T


def solution(mesh):
    in_specs = (
        P("comp", "prompt"),
        P("comp", "prompt"),
        P("comp", "prompt"),
        P("prompt", None, None),
        P("prompt", None, None),
        P("prompt", None),
        P("prompt", None),
        P("comp", None),
        P("comp", None),
        P("comp"),
    )
    out_specs = (
        P(("prompt", "comp"), None, None),
        P(("prompt", "comp"), None, None),
        P(("prompt", "comp"), None),
        P(("prompt", "comp"), None),
        P("comp", "prompt"),
        P("comp", "prompt"),
    )
    return jax.shard_map(local, mesh=mesh, in_specs=in_specs, out_specs=out_specs, check_vma=False)
```

```python
import functools

import jax
import jax.numpy as jnp
from jax import lax
from jax.experimental import pallas as pl
from jax.experimental.pallas import tpu as pltpu
from jax.sharding import PartitionSpec as P

f32 = jnp.float32
bf16 = jnp.bfloat16
LOG2E = 1.4426950408889634

ROWS = 128
SLEN = 64
LAT = 512
ROPE = 64
NOPE = 128
KW = 640
HW = 384
W = 2 * ROWS
PK = 1024
AK = PK + 2 * ROWS
SCALE = 1.0 / (NOPE + ROPE) ** 0.5


def nt(a, b):
    return lax.dot_general(a, b, (((1,), (1,)), ((), ())), preferred_element_type=f32)


def nn(a, b):
    return lax.dot_general(a, b, (((1,), (0,)), ((), ())), preferred_element_type=f32)


def params(mib=60):
    return pltpu.CompilerParams(vmem_limit_bytes=mib * 2**20)


def cost(flops, nbytes):
    return pl.CostEstimate(flops=flops, bytes_accessed=nbytes, transcendentals=0)


VM = pl.BlockSpec(memory_space=pltpu.VMEM)
SM = pl.BlockSpec(memory_space=pltpu.SMEM)


def keys_kernel(lat, rope_t, kv):
    core = lax.axis_index("comp") % 2
    x = jnp.concatenate(
        [lat[...].astype(f32), rope_t[...].astype(f32).T, jnp.zeros((ROWS, KW - LAT - ROPE), f32)],
        axis=1,
    ).reshape(8, 2, 8, KW)
    x = jnp.where(core == 0, x[:, 0], x[:, 1]).reshape(64, KW).astype(bf16)
    for k in range(8):
        kv[k] = x


def keys(lat, rope_t):
    return pl.pallas_call(
        keys_kernel,
        out_shape=jax.ShapeDtypeStruct((8, 64, KW), bf16),
        in_specs=[VM, VM],
        out_specs=VM,
        compiler_params=params(),
        name="keys",
    )(lat, rope_t)


def prep_kernel(info, lens, *refs):
    core = info[0]
    row = lax.broadcasted_iota(jnp.int32, (ROWS, 1), 0)
    limit = jnp.where(row < SLEN, lens[0], lens[1])
    valid = (row % SLEN) < limit
    lane = lax.broadcasted_iota(jnp.int32, (ROWS, 2 * ROPE), 1)
    keep, send, ww, done = refs[-4:]
    done[...] = jnp.zeros_like(done)
    for h in range(2):
        qn_k, qn_s, do_k, do_s, qr, wk, wv = refs[7 * h : 7 * h + 7]
        tile = qr[...].astype(f32)
        flipped = pltpu.roll(tile, ROPE, 1)
        for out, qn, do, par in ((keep, qn_k, do_k, core), (send, qn_s, do_s, 1 - core)):
            out[h, :, 0:NOPE] = qn[...]
            x = jnp.where(lane < ROPE, jnp.where(par == 0, tile, flipped), 0.0)
            out[h, :, NOPE : 2 * NOPE] = x.astype(bf16)
            g = do[...]
            out[h, :, 2 * NOPE : HW] = jnp.where(valid, g, jnp.zeros_like(g))
        ww[h, 0:NOPE] = wk[0]
        ww[h, NOPE : 2 * NOPE] = wv[0].T


def own_kernel(clat, crop_t, after, out):
    out[:, 0:LAT] = clat[...]
    pad = jnp.zeros((ROWS, KW - LAT - ROPE), bf16)
    crop = crop_t[...].astype(f32).T.astype(bf16)
    out[:, LAT:KW] = jnp.concatenate([crop, pad], axis=1)


def own_keys(clat, crop_t, after):
    return pl.pallas_call(
        own_kernel,
        out_shape=jax.ShapeDtypeStruct((ROWS, KW), bf16),
        in_specs=[VM, VM, pl.BlockSpec(memory_space=pl.ANY)],
        out_specs=VM,
        compiler_params=params(4),
        cost_estimate=cost(3 * 10**9, 4 * 2**20),
        name="own_keys",
    )(clat, crop_t, after)


def prep(info, lens, qn, qr, do, w_uk, w_uv):
    def head(i, info, flip):
        core = info[0]
        return 2 * info[5 + i] + (1 - core if flip else core)

    in_specs, ops = [], []
    for h in range(2):

        def cols(flip, h=h):
            return pl.BlockSpec((ROWS, NOPE), lambda i, info, lens: (0, head(2 * i + h, info, flip)))

        def weight(a, b, h=h):
            return pl.BlockSpec(
                (1, a, b), lambda i, info, lens: (head(2 * i + h, info, False), 0, 0)
            )

        def pair(h=h):
            return pl.BlockSpec((ROWS, 2 * ROPE), lambda i, info, lens: (0, info[5 + 2 * i + h]))

        in_specs += [cols(False), cols(True), cols(False), cols(True), pair()]
        in_specs += [weight(NOPE, LAT), weight(LAT, NOPE)]
        ops += [qn, qn, do, do, qr, w_uk, w_uv]
    out = pl.BlockSpec((2, ROWS, HW), lambda i, info, lens: (i, 0, 0))
    return pl.pallas_call(
        prep_kernel,
        out_shape=(
            jax.ShapeDtypeStruct((8, ROWS, HW), bf16),
            jax.ShapeDtypeStruct((8, ROWS, HW), bf16),
            jax.ShapeDtypeStruct((8, 2 * NOPE, LAT), bf16),
            jax.ShapeDtypeStruct((8, 128), f32),
        ),
        grid_spec=pltpu.PrefetchScalarGridSpec(
            num_scalar_prefetch=2,
            grid=(4,),
            in_specs=in_specs,
            out_specs=(
                out,
                out,
                pl.BlockSpec((2, 2 * NOPE, LAT), lambda i, info, lens: (i, 0, 0)),
                pl.BlockSpec((8, 128), lambda i, info, lens: (0, 0)),
            ),
        ),
        compiler_params=params(),
        cost_estimate=cost(10**9, 4 * 2**20),
        name="prep",
    )(info, lens, *ops)


HPS = 2
STEPS = 2


def attend_kernel(last, *refs):
    refs = list(refs)

    def take(n):
        return [refs.pop(0) for _ in range(n)]

    kva, kvb, ckeep, crecv, keep, recv, ww = take(7)
    if last:
        (acc,) = take(1)
        rest, stay, give_a, give_b, give_c = take(5)
    else:
        plus, minus, acc = take(3)
    kall, kt, kx, s_ref, dp_ref, pb, ds, xy, rop = take(9)
    step = pl.program_id(0)
    CH = 128
    NC = (PK + ROWS) // CH

    @pl.when(step == 0)
    def _():
        for at, ref in ((0, kva), (512, kvb)):
            kall[at : at + 512] = ref[:, 0:LAT]
            for h in range(HPS):
                kx[h, at : at + 512, 128:256] = ref[:, LAT:KW]
        for at, ref in ((PK, ckeep), (PK + ROWS, crecv)):
            kall[at : at + ROWS] = ref[:, 0:LAT]
            for h in range(HPS):
                kx[h, at : at + ROWS, 128:256] = ref[:, LAT:KW]
        for b in range(AK // 256):
            kt[:, b * 256 : b * 256 + 256] = kall[b * 256 : b * 256 + 256, :].T
        zero = jnp.zeros((ROWS, ROWS), bf16)
        for ref in (pb, ds):
            for h in range(HPS):
                ref[h, PK : PK + ROWS, ROWS:W] = zero
                ref[h, PK + ROWS : AK, 0:ROWS] = zero
        rop[...] = acc[:, LAT:KW] if last else jnp.zeros_like(rop)

    iu = lax.broadcasted_iota(jnp.int32, (ROWS, W), 0)
    it = lax.broadcasted_iota(jnp.int32, (ROWS, W), 1) % ROWS
    seen = ((iu // SLEN) == (it // SLEN)) & (iu <= it)
    queries = []
    for h in range(HPS):
        at = pl.multiple_of((step * HPS + h) * W, W)
        r = nt(kall[...], ww[pl.ds(at, W), :])
        kx[h, :, 0:128] = r[:, 0:128].astype(bf16)
        kx[h, :, 256:384] = r[:, 128:256].astype(bf16)
    for h in range(HPS):
        qx = jnp.concatenate([keep[h, :, 0:256], recv[h, :, 0:256]], axis=0)
        g = jnp.concatenate([keep[h, :, 256:HW], recv[h, :, 256:HW]], axis=0)
        queries.append((qx, g))
        s_ref[h, 0:PK] = nt(kx[h, 0:PK, 0:256], qx)
        own = nt(kx[h, PK:AK, 0:256], qx)
        own = jnp.concatenate([own[0:ROWS, 0:ROWS], own[ROWS:W, ROWS:W]], axis=1)
        s_ref[h, PK : PK + ROWS] = jnp.where(seen, own, -jnp.inf)
        dp_ref[h, 0:PK] = nt(kx[h, 0:PK, 256:384], g)
        own = nt(kx[h, PK:AK, 256:384], g)
        dp_ref[h, PK : PK + ROWS] = jnp.concatenate(
            [own[0:ROWS, 0:ROWS], own[ROWS:W, ROWS:W]], axis=1
        )
    both = []
    for h in range(HPS):
        qx, g = queries[h]
        top = jnp.full((8, W), -jnp.inf, f32)
        for c in range(NC):
            x = s_ref[h, c * CH : c * CH + CH].reshape(CH // 8, 8, W)
            top = jnp.maximum(top, jnp.max(x, axis=0))
        top = jnp.max(top, axis=0, keepdims=True)
        total = jnp.zeros((8, W), f32)
        delta = jnp.zeros((8, W), f32)
        for c in range(NC):
            cs = slice(c * CH, c * CH + CH)
            e = jnp.exp2((s_ref[h, cs] - top) * (SCALE * LOG2E))
            s_ref[h, cs] = e
            total = total + jnp.sum(e.reshape(CH // 8, 8, W), axis=0)
            delta = delta + jnp.sum((e * dp_ref[h, cs]).reshape(CH // 8, 8, W), axis=0)
        inv = 1.0 / jnp.sum(total, axis=0, keepdims=True)
        delta = jnp.sum(delta, axis=0, keepdims=True) * inv
        cinv = inv * SCALE
        for c in range(NC):
            cs = slice(c * CH, c * CH + CH)
            e = s_ref[h, cs]
            p = (e * inv).astype(bf16)
            d = (e * cinv * (dp_ref[h, cs] - delta)).astype(bf16)
            if c < NC - 1:
                pb[h, cs] = p
                ds[h, cs] = d
            else:
                for ref, x in ((pb, p), (ds, d)):
                    ref[h, PK : PK + ROWS, 0:ROWS] = x[:, 0:ROWS]
                    ref[h, PK + ROWS : AK, ROWS:W] = x[:, ROWS:W]
        x = nn(ds[h], qx)
        rop[...] += x[:, 128:256]
        y = nn(pb[h], g)
        xx = jnp.concatenate([x[:, 0:128].astype(bf16), y.astype(bf16)], axis=1)
        at = pl.multiple_of((step * HPS + h) * W, W)
        xy[:, pl.ds(at, W)] = xx
        both.append(xx)
    for h in range(HPS):
        out = nn(kt[...], both[h]).astype(bf16)
        if last:
            rest[h] = out
        elif h == 0:
            plus[0] = out
        else:
            minus[0] = out

    @pl.when(step == STEPS - 1)
    def _():
        r = nn(xy[...], ww[...])
        if last:
            r = jnp.concatenate([r + acc[:, 0:LAT], rop[...]], axis=1).astype(bf16)
            stay[0:512] = r[0:512]
            stay[512:640] = r[PK : PK + ROWS]
            give_a[...] = r[512:768]
            give_b[...] = r[768:1024]
            give_c[...] = r[PK + ROWS : AK]
        else:
            acc[:, 0:LAT] = r
            acc[:, LAT:KW] = rop[...]


def attend(last, kva, kvb, ckeep, crecv, keep, recv, ww, acc=None):
    base = 2 if last else 0

    def full(a, b):
        return pl.BlockSpec((a, b), lambda s: (0, 0))

    def block(n):
        return pl.BlockSpec((n, LAT, 2 * NOPE), lambda s: (s, 0, 0))

    def shape(n):
        return jax.ShapeDtypeStruct((n, LAT, 2 * NOPE), bf16)

    heads = pl.BlockSpec((HPS, ROWS, HW), lambda s: (base + s, 0, 0))
    ckeys = full(ROWS, KW)
    weights = pl.BlockSpec((STEPS * HPS * W, LAT), lambda s: (base // 2, 0))
    in_specs = [full(512, KW), full(512, KW), ckeys, ckeys, heads, heads, weights]
    ops = [kva, kvb, ckeep, crecv, keep, recv, ww]
    scratch = [
        pltpu.VMEM((AK, LAT), bf16),
        pltpu.VMEM((LAT, AK), bf16),
        pltpu.VMEM((HPS, AK, 384), bf16),
        pltpu.VMEM((HPS, PK + ROWS, W), f32),
        pltpu.VMEM((HPS, PK + ROWS, W), f32),
        pltpu.VMEM((HPS, AK, W), bf16),
        pltpu.VMEM((HPS, AK, W), bf16),
        pltpu.VMEM((AK, STEPS * HPS * W), bf16),
        pltpu.VMEM((AK, 128), f32),
    ]
    if last:
        in_specs.append(full(AK, KW))
        ops.append(acc)
        out_shape = [shape(4)]
        out_specs = [block(2)]
        for n in (640, 256, 256, ROWS):
            out_shape.append(jax.ShapeDtypeStruct((n, KW), bf16))
            out_specs.append(full(n, KW))
    else:
        out_shape = (shape(2), shape(2), jax.ShapeDtypeStruct((AK, KW), f32))
        out_specs = (block(1), block(1), full(AK, KW))
    return pl.pallas_call(
        functools.partial(attend_kernel, last),
        out_shape=out_shape,
        grid=(STEPS,),
        in_specs=in_specs,
        out_specs=out_specs,
        scratch_shapes=scratch,
        compiler_params=params(36),
        cost_estimate=cost(10**10, 10 * 2**20),
        name="attend",
    )(*ops)


YW = 768


def join_kernel(stay, got_a, got_b, got_c, o0, o1, o2, o3):
    y = lax.axis_index("prompt") // 2
    crope = stay[512:640, LAT:KW].astype(f32) + got_c[:, LAT:KW].astype(f32)
    for k, out in enumerate((o0, o1, o2, o3)):
        to = lax.rem(y + k, 4)
        at = pl.multiple_of(to * 128, 128)
        row = pl.ds(at, 128)
        half = pl.ds(pl.multiple_of(lax.rem(to, 2) * 128, 128), 128)
        got = jnp.where(to < 2, got_a[half, :].astype(f32), got_b[half, :].astype(f32))
        x = stay[row, :].astype(f32) + got
        c = stay[512:640, row].astype(f32) + got_c[:, row].astype(f32)
        r = pltpu.roll(crope, lax.rem(KW - LAT + ROPE - 16 * to, KW - LAT), 1)
        lane = lax.broadcasted_iota(jnp.int32, (ROWS, KW - LAT), 1)
        tail = jnp.where(lane < ROPE, x[:, LAT:KW], r)
        out[:, 0:LAT] = x[:, 0:LAT].astype(bf16)
        out[:, LAT:KW] = tail.astype(bf16)
        out[:, KW:YW] = c.astype(bf16)


def join(stay, *got):
    return pl.pallas_call(
        join_kernel,
        out_shape=(jax.ShapeDtypeStruct((128, YW), bf16),) * 4,
        in_specs=[VM] * 4,
        out_specs=(VM,) * 4,
        compiler_params=params(24),
        name="join",
    )(stay, *got)


def sum_y_kernel(a0, a1, a2, a3, out, mine, send):
    xl = lax.axis_index("prompt") % 2
    x = a0[...].astype(f32) + a1[...].astype(f32) + a2[...].astype(f32) + a3[...].astype(f32)
    out[...] = x[:, 0:KW].astype(bf16)
    lane = lax.broadcasted_iota(jnp.int32, (ROWS, 128), 1)
    lat, rope = x[:, KW:YW], x[:, LAT:KW]
    for ref, flip in ((mine, 0), (send, 1)):
        to = xl ^ flip
        c = pltpu.roll(lat, lax.rem(128 - 64 * to, 128), 1)
        r = pltpu.roll(rope, lax.rem(128 - 8 * to, 128), 1)
        ref[...] = jnp.where(lane < 64, c, r).astype(bf16)


def sum_y(*parts):
    return pl.pallas_call(
        sum_y_kernel,
        out_shape=(
            jax.ShapeDtypeStruct((128, KW), bf16),
            jax.ShapeDtypeStruct((ROWS, 128), bf16),
            jax.ShapeDtypeStruct((ROWS, 128), bf16),
        ),
        in_specs=[VM] * 4,
        out_specs=(VM,) * 3,
        compiler_params=params(24),
        name="sum_y",
    )(*parts)


def final_kernel(mine, got, dlat, after, ol, orp, ocl, ocr):
    c = (mine[...].astype(f32) + got[...].astype(f32)).T
    ocl[...] = c[0:64]
    ocr[...] = c[64:72]
    x = jnp.sum(dlat[...].astype(f32).reshape(16, 8, KW), axis=0)
    ol[...] = x[:, 0:LAT]
    orp[...] = x[:, LAT : LAT + ROPE]


def final(mine, got, dlat, after):
    return pl.pallas_call(
        final_kernel,
        out_shape=(
            jax.ShapeDtypeStruct((8, LAT), f32),
            jax.ShapeDtypeStruct((8, ROPE), f32),
            jax.ShapeDtypeStruct((64, ROWS), f32),
            jax.ShapeDtypeStruct((8, ROWS), f32),
        ),
        in_specs=[VM] * 4,
        out_specs=(VM,) * 4,
        compiler_params=params(24),
        name="final",
    )(mine, got, dlat, after)


def ring_kernel(rest, p, m, after, a, b):
    a[...] = (rest[0].astype(f32) + p[0].astype(f32)).astype(bf16)
    b[...] = (rest[1].astype(f32) + m[0].astype(f32)).astype(bf16)


def ring(rest, p, m, after):
    block = jax.ShapeDtypeStruct((LAT, 2 * NOPE), bf16)
    return pl.pallas_call(
        ring_kernel,
        out_shape=(block, block),
        in_specs=[VM] * 3 + [pl.BlockSpec(memory_space=pl.ANY)],
        out_specs=(VM, VM),
        compiler_params=params(24),
        name="ring",
    )(rest, p, m, after)


def pair_kernel(rest, p, m, a, b, mine, send):
    first = rest[2].astype(f32) + m[1].astype(f32) + a[...].astype(f32)
    second = rest[3].astype(f32) + p[1].astype(f32) + b[...].astype(f32)
    own = (lax.axis_index("comp") // 2) % 2 == 0
    mine[...] = jnp.where(own, first, second).astype(bf16)
    send[...] = jnp.where(own, second, first).astype(bf16)


def pair(rest, p, m, a, b):
    block = jax.ShapeDtypeStruct((LAT, 2 * NOPE), bf16)
    return pl.pallas_call(
        pair_kernel,
        out_shape=(block, block),
        in_specs=[VM] * 5,
        out_specs=(VM, VM),
        compiler_params=params(24),
        name="pair",
    )(rest, p, m, a, b)


def weights_kernel(mine, got, dwk, dwv, done):
    done[...] = jnp.zeros_like(done)
    x = mine[...].astype(f32) + got[...].astype(f32)
    dwk[...] = x[:, 0:NOPE].T
    dwv[...] = x[:, NOPE : 2 * NOPE]


def weights(mine, got):
    return pl.pallas_call(
        weights_kernel,
        out_shape=(
            jax.ShapeDtypeStruct((NOPE, LAT), f32),
            jax.ShapeDtypeStruct((LAT, NOPE), f32),
            jax.ShapeDtypeStruct((8, 128), f32),
        ),
        in_specs=[VM, VM],
        out_specs=(VM, VM, VM),
        compiler_params=params(24),
        name="weights",
    )(mine, got)


def local(q_nope, q_rope, d_out, w_uk, w_uv, latent, rope_key, comp_latent, comp_rope, lengths):
    comp = lax.axis_index("comp").astype(jnp.int32)
    prm = lax.axis_index("prompt").astype(jnp.int32)
    z = comp // 4
    far, after, before = (z + 2) % 4, (z + 1) % 4, (z + 3) % 4
    info = jnp.stack(
        [comp % 2, prm // 2, prm % 2, (comp // 2) % 2, z]
        + [2 * far, 2 * far + 1, 2 * after + 1, 2 * before]
        + [2 * after, 2 * before + 1, 2 * z, 2 * z + 1]
    )
    swap = [(c, c ^ 1) for c in range(16)]
    up = [(c, (c + 4) % 16) for c in range(16)]
    down = [(c, (c + 12) % 16) for c in range(16)]
    kv = keys(latent, rope_key.T)
    kva = lax.all_to_all(kv, "prompt", 0, 0, tiled=True).reshape(512, KW)
    keep, send, ww, done = prep(
        info, lengths, q_nope, q_rope, d_out, w_uk, w_uv
    )
    recv = lax.ppermute(send, "comp", swap)
    ckeep = own_keys(comp_latent, comp_rope.T, done)
    crecv = lax.ppermute(ckeep, "comp", swap)
    kvb = lax.ppermute(kva, "comp", swap)
    ops = (kva, kvb, ckeep, crecv, keep, recv, ww.reshape(8 * W, LAT))
    plus, minus, acc = attend(False, *ops)
    plus = lax.ppermute(plus, "comp", up)
    minus = lax.ppermute(minus, "comp", down)
    rest, stay, *give = attend(True, *ops, acc)
    got = [lax.ppermute(x, "comp", swap) for x in give]
    o = join(stay, *got)
    o = [o[0]] + [
        lax.ppermute(o[k], "prompt", [(i, (i + 2 * k) % 8) for i in range(8)]) for k in (1, 2, 3)
    ]
    a, b = ring(rest, plus, minus, o[0])
    a = lax.ppermute(a, "comp", up)
    b = lax.ppermute(b, "comp", down)
    dlat, cmine, csend = sum_y(*o)
    planes = [
        [(2 * y + xl) * 16 + 2 * i + core for xl in range(2) for i in range(8)]
        for y in range(4)
        for core in range(2)
    ]
    cgot = lax.ppermute(csend, "prompt", [(i, i ^ 1) for i in range(8)])
    dlat = lax.all_to_all(
        dlat, ("prompt", "comp"), 0, 0, tiled=True, axis_index_groups=planes
    )
    mine, send = pair(rest, plus, minus, a, b)
    other = lax.ppermute(send, "comp", [(c, c ^ 2) for c in range(16)])
    dwk, dwv, done = weights(mine, other)
    ol, orp, ocl, ocr = final(cmine, cgot, dlat, done)
    return dwk[None], dwv[None], ol, orp, ocl.T, ocr.T


def solution(mesh):
    in_specs = (
        P("comp", "prompt"),
        P("comp", "prompt"),
        P("comp", "prompt"),
        P("prompt", None, None),
        P("prompt", None, None),
        P("prompt", None),
        P("prompt", None),
        P("comp", None),
        P("comp", None),
        P("comp"),
    )
    out_specs = (
        P(("prompt", "comp"), None, None),
        P(("prompt", "comp"), None, None),
        P(("prompt", "comp"), None),
        P(("prompt", "comp"), None),
        P("comp", "prompt"),
        P("comp", "prompt"),
    )
    return jax.shard_map(local, mesh=mesh, in_specs=in_specs, out_specs=out_specs, check_vma=False)
```

```python
import functools

import jax
import jax.numpy as jnp
from jax import lax
from jax.experimental import pallas as pl
from jax.experimental.pallas import tpu as pltpu
from jax.sharding import PartitionSpec as P

f32 = jnp.float32
bf16 = jnp.bfloat16
LOG2E = 1.4426950408889634

ROWS = 128
SLEN = 64
LAT = 512
ROPE = 64
NOPE = 128
KW = 640
HW = 384
W = 2 * ROWS
PK = 1024
AK = PK + 2 * ROWS
SCALE = 1.0 / (NOPE + ROPE) ** 0.5


def nt(a, b):
    return lax.dot_general(a, b, (((1,), (1,)), ((), ())), preferred_element_type=f32)


def nn(a, b):
    return lax.dot_general(a, b, (((1,), (0,)), ((), ())), preferred_element_type=f32)


def params(mib=60):
    return pltpu.CompilerParams(vmem_limit_bytes=mib * 2**20)


def cost(flops, nbytes):
    return pl.CostEstimate(flops=flops, bytes_accessed=nbytes, transcendentals=0)


VM = pl.BlockSpec(memory_space=pltpu.VMEM)
SM = pl.BlockSpec(memory_space=pltpu.SMEM)


def keys_kernel(lat, rope_t, kv):
    core = lax.axis_index("comp") % 2
    x = jnp.concatenate(
        [lat[...].astype(f32), rope_t[...].astype(f32).T, jnp.zeros((ROWS, KW - LAT - ROPE), f32)],
        axis=1,
    ).reshape(8, 2, 8, KW)
    x = jnp.where(core == 0, x[:, 0], x[:, 1]).reshape(64, KW).astype(bf16)
    for k in range(8):
        kv[k] = x


def keys(lat, rope_t):
    return pl.pallas_call(
        keys_kernel,
        out_shape=jax.ShapeDtypeStruct((8, 64, KW), bf16),
        in_specs=[VM, VM],
        out_specs=VM,
        compiler_params=params(),
        name="keys",
    )(lat, rope_t)


def prep_kernel(info, lens, *refs):
    core = info[0]
    row = lax.broadcasted_iota(jnp.int32, (ROWS, 1), 0)
    limit = jnp.where(row < SLEN, lens[0], lens[1])
    valid = (row % SLEN) < limit
    lane = lax.broadcasted_iota(jnp.int32, (ROWS, 2 * ROPE), 1)
    keep, send, ww, done = refs[-4:]
    done[...] = jnp.zeros_like(done)
    for h in range(2):
        qn_k, qn_s, do_k, do_s, qr, wk, wv = refs[7 * h : 7 * h + 7]
        tile = qr[...].astype(f32)
        flipped = pltpu.roll(tile, ROPE, 1)
        for out, qn, do, par in ((keep, qn_k, do_k, core), (send, qn_s, do_s, 1 - core)):
            out[h, :, 0:NOPE] = qn[...]
            x = jnp.where(lane < ROPE, jnp.where(par == 0, tile, flipped), 0.0)
            out[h, :, NOPE : 2 * NOPE] = x.astype(bf16)
            g = do[...]
            out[h, :, 2 * NOPE : HW] = jnp.where(valid, g, jnp.zeros_like(g))
        ww[h, 0:NOPE] = wk[0]
        ww[h, NOPE : 2 * NOPE] = wv[0].T


def own_kernel(clat, crop_t, after, out):
    out[:, 0:LAT] = clat[...]
    pad = jnp.zeros((ROWS, KW - LAT - ROPE), bf16)
    crop = crop_t[...].astype(f32).T.astype(bf16)
    out[:, LAT:KW] = jnp.concatenate([crop, pad], axis=1)


def own_keys(clat, crop_t, after):
    return pl.pallas_call(
        own_kernel,
        out_shape=jax.ShapeDtypeStruct((ROWS, KW), bf16),
        in_specs=[VM, VM, pl.BlockSpec(memory_space=pl.ANY)],
        out_specs=VM,
        compiler_params=params(4),
        cost_estimate=cost(3 * 10**9, 4 * 2**20),
        name="own_keys",
    )(clat, crop_t, after)


def prep(info, lens, qn, qr, do, w_uk, w_uv):
    def head(i, info, flip):
        core = info[0]
        return 2 * info[5 + i] + (1 - core if flip else core)

    in_specs, ops = [], []
    for h in range(2):

        def cols(flip, h=h):
            return pl.BlockSpec((ROWS, NOPE), lambda i, info, lens: (0, head(2 * i + h, info, flip)))

        def weight(a, b, h=h):
            return pl.BlockSpec(
                (1, a, b), lambda i, info, lens: (head(2 * i + h, info, False), 0, 0)
            )

        def pair(h=h):
            return pl.BlockSpec((ROWS, 2 * ROPE), lambda i, info, lens: (0, info[5 + 2 * i + h]))

        in_specs += [cols(False), cols(True), cols(False), cols(True), pair()]
        in_specs += [weight(NOPE, LAT), weight(LAT, NOPE)]
        ops += [qn, qn, do, do, qr, w_uk, w_uv]
    out = pl.BlockSpec((2, ROWS, HW), lambda i, info, lens: (i, 0, 0))
    return pl.pallas_call(
        prep_kernel,
        out_shape=(
            jax.ShapeDtypeStruct((8, ROWS, HW), bf16),
            jax.ShapeDtypeStruct((8, ROWS, HW), bf16),
            jax.ShapeDtypeStruct((8, 2 * NOPE, LAT), bf16),
            jax.ShapeDtypeStruct((8, 128), f32),
        ),
        grid_spec=pltpu.PrefetchScalarGridSpec(
            num_scalar_prefetch=2,
            grid=(4,),
            in_specs=in_specs,
            out_specs=(
                out,
                out,
                pl.BlockSpec((2, 2 * NOPE, LAT), lambda i, info, lens: (i, 0, 0)),
                pl.BlockSpec((8, 128), lambda i, info, lens: (0, 0)),
            ),
        ),
        compiler_params=params(),
        cost_estimate=cost(10**9, 4 * 2**20),
        name="prep",
    )(info, lens, *ops)


HPS = 2
STEPS = 2


def attend_kernel(last, *refs):
    refs = list(refs)

    def take(n):
        return [refs.pop(0) for _ in range(n)]

    kva, kvb, ckeep, crecv, keep, recv, ww = take(7)
    if last:
        (acc,) = take(1)
        rest, stay, give_a, give_b, give_c = take(5)
    else:
        plus, minus, acc = take(3)
    kall, kt, kx, s_ref, dp_ref, pb, ds, xy, rop = take(9)
    base = 4 if last else 0
    CH = 128
    NC = (PK + ROWS) // CH

    for at, ref in ((0, kva), (512, kvb)):
        kall[at : at + 512] = ref[:, 0:LAT]
        for h in range(HPS):
            kx[h, at : at + 512, 128:256] = ref[:, LAT:KW]
    for at, ref in ((PK, ckeep), (PK + ROWS, crecv)):
        kall[at : at + ROWS] = ref[:, 0:LAT]
        for h in range(HPS):
            kx[h, at : at + ROWS, 128:256] = ref[:, LAT:KW]
    for b in range(AK // 256):
        kt[:, b * 256 : b * 256 + 256] = kall[b * 256 : b * 256 + 256, :].T
    zero = jnp.zeros((ROWS, ROWS), bf16)
    for ref in (pb, ds):
        for h in range(HPS):
            ref[h, PK : PK + ROWS, ROWS:W] = zero
            ref[h, PK + ROWS : AK, 0:ROWS] = zero
    rop[...] = acc[:, LAT:KW] if last else jnp.zeros_like(rop)

    iu = lax.broadcasted_iota(jnp.int32, (ROWS, W), 0)
    it = lax.broadcasted_iota(jnp.int32, (ROWS, W), 1) % ROWS
    seen = ((iu // SLEN) == (it // SLEN)) & (iu <= it)
    for step in range(STEPS):
        queries = []
        for h in range(HPS):
            at = (step * HPS + h) * W
            r = nt(kall[...], ww[base * W + at : base * W + at + W, :])
            kx[h, :, 0:128] = r[:, 0:128].astype(bf16)
            kx[h, :, 256:384] = r[:, 128:256].astype(bf16)
        for h in range(HPS):
            qx = jnp.concatenate([keep[base + step * HPS + h, :, 0:256], recv[base + step * HPS + h, :, 0:256]], axis=0)
            g = jnp.concatenate([keep[base + step * HPS + h, :, 256:HW], recv[base + step * HPS + h, :, 256:HW]], axis=0)
            queries.append((qx, g))
            s_ref[h, 0:PK] = nt(kx[h, 0:PK, 0:256], qx)
            own = nt(kx[h, PK:AK, 0:256], qx)
            own = jnp.concatenate([own[0:ROWS, 0:ROWS], own[ROWS:W, ROWS:W]], axis=1)
            s_ref[h, PK : PK + ROWS] = jnp.where(seen, own, -jnp.inf)
            dp_ref[h, 0:PK] = nt(kx[h, 0:PK, 256:384], g)
            own = nt(kx[h, PK:AK, 256:384], g)
            dp_ref[h, PK : PK + ROWS] = jnp.concatenate(
                [own[0:ROWS, 0:ROWS], own[ROWS:W, ROWS:W]], axis=1
            )
        both = []
        for h in range(HPS):
            qx, g = queries[h]
            top = jnp.full((8, W), -jnp.inf, f32)
            for c in range(NC):
                x = s_ref[h, c * CH : c * CH + CH].reshape(CH // 8, 8, W)
                top = jnp.maximum(top, jnp.max(x, axis=0))
            top = jnp.max(top, axis=0, keepdims=True)
            total = jnp.zeros((8, W), f32)
            delta = jnp.zeros((8, W), f32)
            for c in range(NC):
                cs = slice(c * CH, c * CH + CH)
                e = jnp.exp2((s_ref[h, cs] - top) * (SCALE * LOG2E))
                s_ref[h, cs] = e
                total = total + jnp.sum(e.reshape(CH // 8, 8, W), axis=0)
                delta = delta + jnp.sum((e * dp_ref[h, cs]).reshape(CH // 8, 8, W), axis=0)
            inv = 1.0 / jnp.sum(total, axis=0, keepdims=True)
            delta = jnp.sum(delta, axis=0, keepdims=True) * inv
            cinv = inv * SCALE
            for c in range(NC):
                cs = slice(c * CH, c * CH + CH)
                e = s_ref[h, cs]
                p = (e * inv).astype(bf16)
                d = (e * cinv * (dp_ref[h, cs] - delta)).astype(bf16)
                if c < NC - 1:
                    pb[h, cs] = p
                    ds[h, cs] = d
                else:
                    for ref, x in ((pb, p), (ds, d)):
                        ref[h, PK : PK + ROWS, 0:ROWS] = x[:, 0:ROWS]
                        ref[h, PK + ROWS : AK, ROWS:W] = x[:, ROWS:W]
            x = nn(ds[h], qx)
            rop[...] += x[:, 128:256]
            y = nn(pb[h], g)
            xx = jnp.concatenate([x[:, 0:128].astype(bf16), y.astype(bf16)], axis=1)
            at = (step * HPS + h) * W
            xy[:, at : at + W] = xx
            both.append(xx)
        for h in range(HPS):
            out = nn(kt[...], both[h]).astype(bf16)
            if last:
                rest[step * HPS + h] = out
            elif h == 0:
                plus[step] = out
            else:
                minus[step] = out

    r = nn(xy[...], ww[base * W : (base + 4) * W, :])
    if last:
        r = jnp.concatenate([r + acc[:, 0:LAT], rop[...]], axis=1).astype(bf16)
        stay[0:512] = r[0:512]
        stay[512:640] = r[PK : PK + ROWS]
        give_a[...] = r[512:768]
        give_b[...] = r[768:1024]
        give_c[...] = r[PK + ROWS : AK]
    else:
        acc[:, 0:LAT] = r
        acc[:, LAT:KW] = rop[...]


def attend(last, kva, kvb, ckeep, crecv, keep, recv, ww, acc=None):
    def shape(n):
        return jax.ShapeDtypeStruct((n, LAT, 2 * NOPE), bf16)

    ops = [kva, kvb, ckeep, crecv, keep, recv, ww]
    scratch = [
        pltpu.VMEM((AK, LAT), bf16),
        pltpu.VMEM((LAT, AK), bf16),
        pltpu.VMEM((HPS, AK, 384), bf16),
        pltpu.VMEM((HPS, PK + ROWS, W), f32),
        pltpu.VMEM((HPS, PK + ROWS, W), f32),
        pltpu.VMEM((HPS, AK, W), bf16),
        pltpu.VMEM((HPS, AK, W), bf16),
        pltpu.VMEM((AK, STEPS * HPS * W), bf16),
        pltpu.VMEM((AK, 128), f32),
    ]
    if last:
        ops.append(acc)
        out_shape = [shape(4)]
        for n in (640, 256, 256, ROWS):
            out_shape.append(jax.ShapeDtypeStruct((n, KW), bf16))
    else:
        out_shape = [shape(2), shape(2), jax.ShapeDtypeStruct((AK, KW), f32)]
    return pl.pallas_call(
        functools.partial(attend_kernel, last),
        out_shape=out_shape,
        in_specs=[VM] * len(ops),
        out_specs=[VM] * len(out_shape),
        scratch_shapes=scratch,
        compiler_params=params(30),
        cost_estimate=cost(10**10, 10 * 2**20),
        name="attend",
    )(*ops)


YW = 768


def join_kernel(stay, got_a, got_b, got_c, o0, o1, o2, o3):
    y = lax.axis_index("prompt") // 2
    crope = stay[512:640, LAT:KW].astype(f32) + got_c[:, LAT:KW].astype(f32)
    for k, out in enumerate((o0, o1, o2, o3)):
        to = lax.rem(y + k, 4)
        at = pl.multiple_of(to * 128, 128)
        row = pl.ds(at, 128)
        half = pl.ds(pl.multiple_of(lax.rem(to, 2) * 128, 128), 128)
        got = jnp.where(to < 2, got_a[half, :].astype(f32), got_b[half, :].astype(f32))
        x = stay[row, :].astype(f32) + got
        c = stay[512:640, row].astype(f32) + got_c[:, row].astype(f32)
        r = pltpu.roll(crope, lax.rem(KW - LAT + ROPE - 16 * to, KW - LAT), 1)
        lane = lax.broadcasted_iota(jnp.int32, (ROWS, KW - LAT), 1)
        tail = jnp.where(lane < ROPE, x[:, LAT:KW], r)
        out[:, 0:LAT] = x[:, 0:LAT].astype(bf16)
        out[:, LAT:KW] = tail.astype(bf16)
        out[:, KW:YW] = c.astype(bf16)


def join(stay, *got):
    return pl.pallas_call(
        join_kernel,
        out_shape=(jax.ShapeDtypeStruct((128, YW), bf16),) * 4,
        in_specs=[VM] * 4,
        out_specs=(VM,) * 4,
        compiler_params=params(24),
        name="join",
    )(stay, *got)


def sum_y_kernel(a0, a1, a2, a3, out, mine, send):
    xl = lax.axis_index("prompt") % 2
    x = a0[...].astype(f32) + a1[...].astype(f32) + a2[...].astype(f32) + a3[...].astype(f32)
    out[...] = x[:, 0:KW].astype(bf16)
    lane = lax.broadcasted_iota(jnp.int32, (ROWS, 128), 1)
    lat, rope = x[:, KW:YW], x[:, LAT:KW]
    for ref, flip in ((mine, 0), (send, 1)):
        to = xl ^ flip
        c = pltpu.roll(lat, lax.rem(128 - 64 * to, 128), 1)
        r = pltpu.roll(rope, lax.rem(128 - 8 * to, 128), 1)
        ref[...] = jnp.where(lane < 64, c, r).astype(bf16)


def sum_y(*parts):
    return pl.pallas_call(
        sum_y_kernel,
        out_shape=(
            jax.ShapeDtypeStruct((128, KW), bf16),
            jax.ShapeDtypeStruct((ROWS, 128), bf16),
            jax.ShapeDtypeStruct((ROWS, 128), bf16),
        ),
        in_specs=[VM] * 4,
        out_specs=(VM,) * 3,
        compiler_params=params(24),
        name="sum_y",
    )(*parts)


def final_kernel(mine, got, dlat, ol, orp, ocl, ocr):
    c = (mine[...].astype(f32) + got[...].astype(f32)).T
    ocl[...] = c[0:64]
    ocr[...] = c[64:72]
    x = jnp.sum(dlat[...].astype(f32).reshape(16, 8, KW), axis=0)
    ol[...] = x[:, 0:LAT]
    orp[...] = x[:, LAT : LAT + ROPE]


def final(mine, got, dlat):
    return pl.pallas_call(
        final_kernel,
        out_shape=(
            jax.ShapeDtypeStruct((8, LAT), f32),
            jax.ShapeDtypeStruct((8, ROPE), f32),
            jax.ShapeDtypeStruct((64, ROWS), f32),
            jax.ShapeDtypeStruct((8, ROWS), f32),
        ),
        in_specs=[VM] * 3,
        out_specs=(VM,) * 4,
        compiler_params=params(24),
        name="final",
    )(mine, got, dlat)


def ring_kernel(rest, p, m, after, a, b):
    a[...] = (rest[0].astype(f32) + p[0].astype(f32)).astype(bf16)
    b[...] = (rest[1].astype(f32) + m[0].astype(f32)).astype(bf16)


def ring(rest, p, m, after):
    block = jax.ShapeDtypeStruct((LAT, 2 * NOPE), bf16)
    return pl.pallas_call(
        ring_kernel,
        out_shape=(block, block),
        in_specs=[VM] * 3 + [pl.BlockSpec(memory_space=pl.ANY)],
        out_specs=(VM, VM),
        compiler_params=params(24),
        name="ring",
    )(rest, p, m, after)


def pair_kernel(rest, p, m, a, b, mine, send):
    first = rest[2].astype(f32) + m[1].astype(f32) + a[...].astype(f32)
    second = rest[3].astype(f32) + p[1].astype(f32) + b[...].astype(f32)
    own = (lax.axis_index("comp") // 2) % 2 == 0
    mine[...] = jnp.where(own, first, second).astype(bf16)
    send[...] = jnp.where(own, second, first).astype(bf16)


def pair(rest, p, m, a, b):
    block = jax.ShapeDtypeStruct((LAT, 2 * NOPE), bf16)
    return pl.pallas_call(
        pair_kernel,
        out_shape=(block, block),
        in_specs=[VM] * 5,
        out_specs=(VM, VM),
        compiler_params=params(24),
        name="pair",
    )(rest, p, m, a, b)


def weights_kernel(mine, got, dwk, dwv):
    x = mine[...].astype(f32) + got[...].astype(f32)
    dwk[...] = x[:, 0:NOPE].T
    dwv[...] = x[:, NOPE : 2 * NOPE]


def weights(mine, got):
    return pl.pallas_call(
        weights_kernel,
        out_shape=(
            jax.ShapeDtypeStruct((NOPE, LAT), f32),
            jax.ShapeDtypeStruct((LAT, NOPE), f32),
        ),
        in_specs=[VM, VM],
        out_specs=(VM, VM),
        compiler_params=params(24),
        name="weights",
    )(mine, got)


def local(q_nope, q_rope, d_out, w_uk, w_uv, latent, rope_key, comp_latent, comp_rope, lengths):
    comp = lax.axis_index("comp").astype(jnp.int32)
    prm = lax.axis_index("prompt").astype(jnp.int32)
    z = comp // 4
    far, after, before = (z + 2) % 4, (z + 1) % 4, (z + 3) % 4
    info = jnp.stack(
        [comp % 2, prm // 2, prm % 2, (comp // 2) % 2, z]
        + [2 * far, 2 * far + 1, 2 * after + 1, 2 * before]
        + [2 * after, 2 * before + 1, 2 * z, 2 * z + 1]
    )
    swap = [(c, c ^ 1) for c in range(16)]
    up = [(c, (c + 4) % 16) for c in range(16)]
    down = [(c, (c + 12) % 16) for c in range(16)]
    kv = keys(latent, rope_key.T)
    kva = lax.all_to_all(kv, "prompt", 0, 0, tiled=True).reshape(512, KW)
    keep, send, ww, done = prep(
        info, lengths, q_nope, q_rope, d_out, w_uk, w_uv
    )
    recv = lax.ppermute(send, "comp", swap)
    ckeep = own_keys(comp_latent, comp_rope.T, done)
    crecv = lax.ppermute(ckeep, "comp", swap)
    kvb = lax.ppermute(kva, "comp", swap)
    ops = (kva, kvb, ckeep, crecv, keep, recv, ww.reshape(8 * W, LAT))
    plus, minus, acc = attend(False, *ops)
    plus = lax.ppermute(plus, "comp", up)
    minus = lax.ppermute(minus, "comp", down)
    rest, stay, *give = attend(True, *ops, acc)
    got = [lax.ppermute(x, "comp", swap) for x in give]
    o = join(stay, *got)
    o = [o[0]] + [
        lax.ppermute(o[k], "prompt", [(i, (i + 2 * k) % 8) for i in range(8)]) for k in (1, 2, 3)
    ]
    a, b = ring(rest, plus, minus, o[0])
    a = lax.ppermute(a, "comp", up)
    b = lax.ppermute(b, "comp", down)
    dlat, cmine, csend = sum_y(*o)
    planes = [
        [(2 * y + xl) * 16 + 2 * i + core for xl in range(2) for i in range(8)]
        for y in range(4)
        for core in range(2)
    ]
    cgot = lax.ppermute(csend, "prompt", [(i, i ^ 1) for i in range(8)])
    dlat = lax.all_to_all(
        dlat, ("prompt", "comp"), 0, 0, tiled=True, axis_index_groups=planes
    )
    mine, send = pair(rest, plus, minus, a, b)
    other = lax.ppermute(send, "comp", [(c, c ^ 2) for c in range(16)])
    dwk, dwv = weights(mine, other)
    ol, orp, ocl, ocr = final(cmine, cgot, dlat)
    return dwk[None], dwv[None], ol, orp, ocl.T, ocr.T


def solution(mesh):
    in_specs = (
        P("comp", "prompt"),
        P("comp", "prompt"),
        P("comp", "prompt"),
        P("prompt", None, None),
        P("prompt", None, None),
        P("prompt", None),
        P("prompt", None),
        P("comp", None),
        P("comp", None),
        P("comp"),
    )
    out_specs = (
        P(("prompt", "comp"), None, None),
        P(("prompt", "comp"), None, None),
        P(("prompt", "comp"), None),
        P(("prompt", "comp"), None),
        P("comp", "prompt"),
        P("comp", "prompt"),
    )
    return jax.shard_map(local, mesh=mesh, in_specs=in_specs, out_specs=out_specs, check_vma=False)
```
